32 devices in a mesh: groups: 2 (over x), wide: 16 (over z, y, core).
Axes of the slice: x: 2, y: 2, z: 4, core: 2. Of those that a mesh axis runs over, the one named last changes fastest.
Arguments:
- queries: bfloat16 [4096, 4096], P(('groups', 'wide')), parts along dimension 0, may hold values from -64 to 64
- first_keys: bfloat16 [4096, 4096], P(('groups', 'wide')), parts along dimension 0, may hold values from -4 to 4
- first_values: bfloat16 [4096, 4096], P(('groups', 'wide')), parts along dimension 0, may hold values from -6 to 6
- second_keys: bfloat16 [4096, 4096], P(('groups', 'wide')), parts along dimension 0, may hold values from -4 to 4
- second_values: bfloat16 [4096, 4096], P(('groups', 'wide')), parts along dimension 0, may hold values from -6 to 6
- out_weight: bfloat16 [4096, 2048], P('wide'), may hold values from -0.09375 to 0.09375
- norm_gain: float32 [2048], replicated, may hold values from 0.1 to 1.9
- gate_weight: bfloat16 [32, 2048, 768], P('wide'), may hold values from -0.125 to 0.125
- up_weight: bfloat16 [32, 2048, 768], P('wide'), may hold values from -0.125 to 0.125
- down_weight: bfloat16 [32, 768, 2048], P('wide'), may hold values from -0.21875 to 0.21875
- routes: int32 [4096, 4], P(('groups', 'wide')), parts along dimension 0, may hold values from 0 to 255, as said below
- route_weights: float32 [4096, 4], P(('groups', 'wide')), parts along dimension 0, may hold values from 0.2 to 1
Outputs:
- layer_out: bfloat16 [4096, 2048], P(('groups', 'wide')), parts along dimension 0
The draws below stay inside these ranges and needn't reach their ends.
There are 2 independent parts, one for each index of `groups`. The reference program is written for one: setup_inputs(seed, part) draws one part's arguments, and reference() takes and returns one part's arrays. A program takes and returns all parts, laid end to end along the dimension named above; an argument that names none is the same for every part. Nothing has to cross between parts.
Inputs may be any that keep to these rules, and one draw needn't show every extreme that they name: `routes`: each token names four different experts. Every expert is named by exactly 32 tokens of the sequence, and by at most 4 tokens among the rows of one device; each expert is named exactly 4 times by the rows of some device.
All inputs are finite; a program needn't handle non-finite values.
Results may differ from the reference program's by a relative error of at most 0.03.
Values may be sent and summed in bfloat16 or wider, within the bound.
A program may use at most 192 MiB of HBM per device.

```python
import math
import jax
import jax.numpy as jnp
from jax import lax

TOK_DEV = 128
HEADS = 32
HEAD_DIM = 128
WIN_KEYS = 512
WIN_PAIRS = 12
D = 2048
FF = 768
EXPERTS = 256
FLIGHT_DEV = 2
SEQ = 2048
FLIGHT = 32
N_WIDE = 16


def simplex_fields(key):
    field_shape = (SEQ, HEADS, HEAD_DIM)
    query_field = 3.0 * jax.random.truncated_normal(jax.random.fold_in(key, 101), -6.0, 6.0, field_shape)
    first_field = jax.random.truncated_normal(jax.random.fold_in(key, 102), -4.0, 4.0, field_shape)
    second_field = jax.random.truncated_normal(jax.random.fold_in(key, 103), -4.0, 4.0, field_shape)
    flat_shape = (SEQ, HEADS * HEAD_DIM)
    return (query_field.reshape(flat_shape), first_field.reshape(flat_shape), second_field.reshape(flat_shape))


def draw_queries(key, part):
    return simplex_fields(key)[0].astype(jnp.bfloat16)


def draw_first_keys(key, part):
    return simplex_fields(key)[1].astype(jnp.bfloat16)


def draw_second_keys(key, part):
    return simplex_fields(key)[2].astype(jnp.bfloat16)


def draw_routes(key, part):
    pair_count = SEQ // (2 * TOK_DEV)
    subkeys = jax.random.split(jax.random.fold_in(key, 201), pair_count)
    orders = jax.vmap(lambda subkey: jax.random.permutation(subkey, EXPERTS))(subkeys)
    halves = orders.reshape(2 * pair_count, EXPERTS // 2)
    columns = jnp.arange(4 * TOK_DEV) % (EXPERTS // 2)
    return halves[:, columns].reshape(SEQ, 4).astype(jnp.int32)


def steps_of(rng, dims, cuts, least, high):
    def one(dim, blocks):
        steps = jax.random.uniform(jax.random.fold_in(jax.random.fold_in(rng, 6), dim), (blocks,), jnp.float32, least / len(cuts), high / len(cuts))
        return jnp.repeat(jnp.exp(steps), dims[dim] // blocks).reshape((-1,) + (1,) * (len(dims) - dim - 1))

    level = one(*cuts[0])
    for cut in cuts[1:]:
        level = level * one(*cut)
    return level


def centred(own_key, extent, width, reach, cuts=(), held_as=jnp.bfloat16):
    level = steps_of(own_key, extent, cuts, -0.22, 0.18) if cuts else 1.0
    values = jax.random.normal(own_key, extent, jnp.float32) * width * level
    return jnp.minimum(jnp.maximum(values, -reach), reach).astype(held_as)


def setup_inputs(seed: int = 0, part: int = 0) -> dict:
    seeds = jax.random.split(jax.random.key(seed), 13)
    part_keys = jax.random.split(jax.random.fold_in(seeds[12], part), 13)
    queries = draw_queries(jax.random.fold_in(jax.random.fold_in(seeds[12], part), 71), part)
    first_keys = draw_first_keys(jax.random.fold_in(jax.random.fold_in(seeds[12], part), 71), part)
    first_values = centred(part_keys[2], (SEQ, HEADS * HEAD_DIM), 1.0, 6.0, ((0, 16),))
    second_keys = draw_second_keys(jax.random.fold_in(jax.random.fold_in(seeds[12], part), 71), part)
    second_values = centred(part_keys[4], (SEQ, HEADS * HEAD_DIM), 1.0, 6.0, ((0, 16),))
    out_weight = centred(seeds[5], (HEADS * HEAD_DIM, D), (HEADS * HEAD_DIM) ** -0.5, 0.09375, ((0, 16),))
    norm_gain = jnp.clip(1.0 + 0.18 * jax.random.normal(seeds[6], (D,), jnp.float32), 0.1, 1.9)
    gate_weight = centred(seeds[7], (FLIGHT, D, FF), D ** -0.5, 0.125, ((0, 16),))
    up_weight = centred(seeds[8], (FLIGHT, D, FF), D ** -0.5, 0.125, ((0, 16),))
    down_weight = centred(seeds[9], (FLIGHT, FF, D), FF ** -0.5, 0.21875, ((0, 16),))
    routes = draw_routes(jax.random.fold_in(jax.random.fold_in(seeds[12], part), 71), part)
    route_weights = jnp.clip(0.2 + 0.8 * jax.random.uniform(part_keys[11], (SEQ, 4), jnp.float32) ** steps_of(part_keys[11], (SEQ, 4), ((0, 16),), -0.2, 0.2), 0.2, 1.0)
    return dict(queries=queries, first_keys=first_keys, first_values=first_values, second_keys=second_keys, second_values=second_values, out_weight=out_weight, norm_gain=norm_gain, gate_weight=gate_weight, up_weight=up_weight, down_weight=down_weight, routes=routes, route_weights=route_weights)


def window_stack(extended, length):
    return jnp.stack([extended[WIN_PAIRS - 1 - offset:WIN_PAIRS - 1 - offset + length] for offset in range(WIN_PAIRS)], axis=1)

def group_attention(pieces, query_start, key_start):
    query_rows, keys_window, values_window, pair_keys_ext, pair_values_ext = pieces
    length = query_rows.shape[0]
    pair_keys = window_stack(pair_keys_ext, length)
    pair_values = window_stack(pair_values_ext, length)
    pair_query = (query_rows[:, None].astype(jnp.float32) * pair_keys.astype(jnp.float32)).astype(jnp.bfloat16)
    scores = jnp.einsum('trgd,lgd->tgrl', pair_query.astype(jnp.float32), keys_window.astype(jnp.float32)) * (1.0 / math.sqrt(HEAD_DIM))
    query_pos = query_start + jnp.arange(length, dtype=jnp.int32)
    key_pos = key_start + jnp.arange(keys_window.shape[0], dtype=jnp.int32)
    offsets = jnp.arange(WIN_PAIRS, dtype=jnp.int32)
    near_mask = (key_pos[None, :] <= query_pos[:, None]) & (key_pos[None, :] > query_pos[:, None] - WIN_KEYS) & (key_pos[None, :] >= 0)
    pair_mask = query_pos[:, None] - offsets[None, :] >= 0
    allowed = near_mask[:, None, None, :] & pair_mask[:, None, :, None]
    scores = jnp.where(allowed, scores, -jnp.inf)
    row_top = lax.optimization_barrier(jnp.max(scores, axis=(2, 3), keepdims=True))
    raised = jnp.exp(scores - row_top)
    weights = (raised / lax.optimization_barrier(jnp.sum(raised, axis=(2, 3), keepdims=True))).astype(jnp.bfloat16)
    partial_value = jnp.einsum('tgrl,lgd->tgrd', weights.astype(jnp.float32), values_window.astype(jnp.float32))
    combined = lax.optimization_barrier(jnp.sum(partial_value * pair_values.transpose(0, 2, 1, 3).astype(jnp.float32), axis=2))
    return combined.astype(jnp.bfloat16)

def reference(queries, first_keys, first_values, second_keys, second_values, out_weight, norm_gain, gate_weight, up_weight, down_weight, routes, route_weights):
    length = TOK_DEV
    reach_blocks = (WIN_KEYS + length - 2) // length
    feature_width = HEADS * HEAD_DIM
    per_step = math.gcd(HEADS, 4)
    groups = HEADS // per_step
    far_zeros = jnp.zeros((reach_blocks * length, feature_width), jnp.bfloat16)
    near_zeros = jnp.zeros((WIN_PAIRS - 1, feature_width), jnp.bfloat16)
    keys_padded = jnp.concatenate([far_zeros, first_keys], axis=0)
    values_padded = jnp.concatenate([far_zeros, first_values], axis=0)
    pair_keys_padded = jnp.concatenate([near_zeros, second_keys], axis=0)
    pair_values_padded = jnp.concatenate([near_zeros, second_values], axis=0)

    def split_heads(matrix):
        return matrix.reshape(matrix.shape[0], groups, per_step, HEAD_DIM).transpose(1, 0, 2, 3)

    def one_block(block_index):
        start_row = block_index * length
        window_rows = (reach_blocks + 1) * length
        pieces = (split_heads(lax.dynamic_slice_in_dim(queries, start_row, length, 0)), split_heads(lax.dynamic_slice_in_dim(keys_padded, start_row, window_rows, 0)), split_heads(lax.dynamic_slice_in_dim(values_padded, start_row, window_rows, 0)), split_heads(lax.dynamic_slice_in_dim(pair_keys_padded, start_row, length + WIN_PAIRS - 1, 0)), split_heads(lax.dynamic_slice_in_dim(pair_values_padded, start_row, length + WIN_PAIRS - 1, 0)))
        key_start = start_row - reach_blocks * length
        result = lax.map(lambda group_pieces: group_attention(group_pieces, start_row, key_start), pieces)
        return result.transpose(1, 0, 2, 3).reshape(length, feature_width)
    attended = lax.map(one_block, jnp.arange(N_WIDE, dtype=jnp.int32)).reshape(SEQ, feature_width)
    projected = jnp.dot(attended, out_weight, preferred_element_type=jnp.float32).astype(jnp.bfloat16)
    wide_proj = projected.astype(jnp.float32)
    normed = (wide_proj * lax.rsqrt(lax.optimization_barrier(jnp.mean(wide_proj * wide_proj, axis=1, keepdims=True)) + 1e-06) * norm_gain).astype(jnp.bfloat16)
    expert_load = 4 * SEQ // EXPERTS

    def expert_step(accum, expert):
        hit_mask = routes == expert
        member = jnp.any(hit_mask, axis=1)
        token_index = jnp.nonzero(member, size=expert_load)[0]
        rows_in = normed[token_index]
        gate_proj = jnp.dot(rows_in, gate_weight[expert], preferred_element_type=jnp.float32)
        upward = jnp.dot(rows_in, up_weight[expert], preferred_element_type=jnp.float32)
        hidden = (jax.nn.silu(gate_proj) * upward).astype(jnp.bfloat16)
        result = jnp.dot(hidden, down_weight[expert], preferred_element_type=jnp.float32).astype(jnp.bfloat16)
        route_scale = lax.optimization_barrier(jnp.sum(jnp.where(hit_mask, route_weights, jnp.float32(0.0)), axis=1))[token_index]
        return (accum.at[token_index].add(route_scale[:, None] * result.astype(jnp.float32)), None)
    expert_sum, unused = lax.scan(expert_step, jnp.zeros((SEQ, D), jnp.float32), jnp.arange(FLIGHT_DEV * N_WIDE, dtype=jnp.int32))
    return (wide_proj + expert_sum).astype(jnp.bfloat16)
```

```python
import functools
import math

import jax
import jax.numpy as jnp
from jax import lax
from jax.experimental import pallas as pl
from jax.experimental.pallas import tpu as pltpu
from jax.sharding import PartitionSpec as P

HEAD_DIM = 128
WIN_KEYS = 512
WIN_PAIRS = 12
CAP = 4
TAIL = 16
FAR = -1e30
SCALE = math.log2(math.e) / math.sqrt(HEAD_DIM)


def head_columns(head):
    return pl.ds(pl.multiple_of(head * HEAD_DIM, HEAD_DIM), HEAD_DIM)


def build_masks(device, length, blocks, keys_ext, pair_query, values_ext, alive):
    row = lax.broadcasted_iota(jnp.int32, (length, length), 0)
    col = lax.broadcasted_iota(jnp.int32, (length, length), 1)
    odd = lax.rem(device, 2)
    distances = (blocks - 1, 2, jnp.where(odd == 1, 1, 3), jnp.where(odd == 1, 3, 1), 0)
    for place, distance in enumerate(distances):
        if place == 0:
            admitted = row > col
        elif place == blocks - 1:
            admitted = row <= col
        else:
            admitted = row >= 0
        admitted = admitted & (device >= distance)
        keys_ext[place * length:(place + 1) * length, HEAD_DIM:] = jnp.where(
            admitted, 0.0, FAR
        ).astype(jnp.bfloat16)
    identity = jnp.where(row == col, 1.0, 0.0).astype(jnp.bfloat16)
    for offset in range(WIN_PAIRS):
        pair_query[offset * length:(offset + 1) * length, HEAD_DIM:] = identity
    values_ext[:, HEAD_DIM:] = jnp.ones((blocks * length, HEAD_DIM), jnp.bfloat16)
    ext_row = lax.broadcasted_iota(jnp.int32, alive.shape, 0)
    alive[...] = jnp.where((ext_row >= TAIL) | (device > 0), 1.0, 0.0)


def score_head(head, query_ref, key_blocks, pair_tail_ref, pair_keys_ref,
               keys_ext, pair_query, pair_ext, scores, tops):
    length = query_ref.shape[0]
    blocks = len(key_blocks)
    cols = head_columns(head)
    pair_ext[0:TAIL, :] = pair_tail_ref[:, cols].astype(jnp.float32)
    pair_ext[TAIL:, :] = pair_keys_ref[:, cols].astype(jnp.float32)
    for place, block in enumerate(key_blocks):
        keys_ext[place * length:(place + 1) * length, :HEAD_DIM] = block[:, cols]
    query = query_ref[:, cols].astype(jnp.float32) * SCALE
    for offset in range(WIN_PAIRS):
        pair_query[offset * length:(offset + 1) * length, :HEAD_DIM] = (
            query * pair_ext[TAIL - offset:TAIL - offset + length, :]
        ).astype(jnp.bfloat16)
    top = None
    total = blocks * length
    for start in range(0, total, 256):
        size = min(256, total - start)
        part = lax.dot_general(
            pair_query[...], keys_ext[start:start + size, :],
            (((1,), (1,)), ((), ())), preferred_element_type=jnp.float32,
        )
        scores[:, start:start + size] = part
        for lane in range(0, size, 128):
            for offset in range(WIN_PAIRS):
                tile = part[offset * length:(offset + 1) * length, lane:lane + 128]
                top = tile if top is None else jnp.maximum(top, tile)
    tops[...] = jnp.broadcast_to(jnp.max(top, axis=1, keepdims=True), tops.shape)


def value_head(head, value_blocks, pair_tail_ref, pair_values_ref,
               values_ext, pair_ext, alive, scores, tops, weights, out_ref):
    length = tops.shape[0]
    blocks = len(value_blocks)
    cols = head_columns(head)
    pair_ext[0:TAIL, :] = pair_tail_ref[:, cols].astype(jnp.float32)
    pair_ext[TAIL:, :] = pair_values_ref[:, cols].astype(jnp.float32)
    for place, block in enumerate(value_blocks):
        values_ext[place * length:(place + 1) * length, :HEAD_DIM] = block[:, cols]
    top = tops[...]
    for offset in range(WIN_PAIRS):
        rows = slice(offset * length, (offset + 1) * length)
        for place in range(blocks):
            lanes = slice(place * length, (place + 1) * length)
            weights[rows, lanes] = jnp.exp2((scores[rows, lanes] - top).astype(jnp.bfloat16))
    product = jnp.dot(weights[...], values_ext[...], preferred_element_type=jnp.float32)
    number = jnp.zeros((length, HEAD_DIM), jnp.float32)
    total = jnp.zeros((length, HEAD_DIM), jnp.float32)
    for offset in range(WIN_PAIRS):
        rows = slice(offset * length, (offset + 1) * length)
        near = slice(TAIL - offset, TAIL - offset + length)
        number += product[rows, :HEAD_DIM] * pair_ext[near, :]
        total += product[rows, HEAD_DIM:] * alive[near, :]
    out_ref[:, cols] = (number / total).astype(out_ref.dtype)


def attention_kernel(query, k0, k1, k2, k3, k4, v0, v1, v2, v3, v4,
                     key_tail, pair_keys, value_tail, pair_values, out,
                     keys_ext, pair_query, values_ext, key_ext, value_ext, alive,
                     scores_a, scores_b, tops_a, tops_b, weights):
    length = query.shape[0]
    heads = query.shape[1] // HEAD_DIM
    key_blocks = (k0, k1, k2, k3, k4)
    value_blocks = (v0, v1, v2, v3, v4)
    device = lax.axis_index("wide")
    build_masks(device, length, len(key_blocks), keys_ext, pair_query, values_ext, alive)

    def score(head, scores, tops):
        score_head(head, query, key_blocks, key_tail, pair_keys,
                   keys_ext, pair_query, key_ext, scores, tops)

    def value(head, scores, tops):
        value_head(head, value_blocks, value_tail, pair_values,
                   values_ext, value_ext, alive, scores, tops, weights, out)

    score(0, scores_a, tops_a)

    def pair(step, carry):
        head = step * 2
        score(head + 1, scores_b, tops_b)
        value(head, scores_a, tops_a)
        score(jnp.minimum(head + 2, heads - 1), scores_a, tops_a)
        value(head + 1, scores_b, tops_b)
        return carry

    lax.fori_loop(0, heads // 2, pair, 0)


def attention(query, key_blocks, value_blocks, key_tail, pair_keys, value_tail, pair_values,
              chunk, width):
    length = query.shape[0]
    blocks = len(key_blocks)
    whole = pl.BlockSpec((length, width), lambda i: (0, chunk))
    sliced = pl.BlockSpec((length, width), lambda i: (0, 0))
    tail = pl.BlockSpec((TAIL, width), lambda i: (0, chunk))
    rows = WIN_PAIRS * length
    keys = blocks * length
    heads = width // HEAD_DIM
    return pl.pallas_call(
        attention_kernel,
        grid=(1,),
        out_shape=jax.ShapeDtypeStruct((length, width), jnp.bfloat16),
        in_specs=[whole] + [sliced] * (2 * blocks) + [tail, whole, tail, whole],
        out_specs=sliced,
        scratch_shapes=[
            pltpu.VMEM((keys, 2 * HEAD_DIM), jnp.bfloat16),
            pltpu.VMEM((rows, 2 * HEAD_DIM), jnp.bfloat16),
            pltpu.VMEM((keys, 2 * HEAD_DIM), jnp.bfloat16),
            pltpu.VMEM((TAIL + length, HEAD_DIM), jnp.float32),
            pltpu.VMEM((TAIL + length, HEAD_DIM), jnp.float32),
            pltpu.VMEM((TAIL + length, HEAD_DIM), jnp.float32),
            pltpu.VMEM((rows, keys), jnp.float32),
            pltpu.VMEM((rows, keys), jnp.float32),
            pltpu.VMEM((length, HEAD_DIM), jnp.float32),
            pltpu.VMEM((length, HEAD_DIM), jnp.float32),
            pltpu.VMEM((rows, keys), jnp.bfloat16),
        ],
        compiler_params=pltpu.CompilerParams(vmem_limit_bytes=40 * 2**20),
        cost_estimate=pl.CostEstimate(
            flops=heads * 8 * rows * keys * HEAD_DIM,
            bytes_accessed=(2 * blocks + 4) * length * width * 2,
            transcendentals=heads * rows * keys,
        ),
    )(query, *key_blocks, *value_blocks, key_tail, pair_keys, value_tail, pair_values)


def spread_blocks(keys, values, devices, device):
    def move(arrays, pairs):
        return lax.ppermute(arrays, "wide", pairs)

    own = (keys, values)
    far = move(own, [(i, i + 4) for i in range(devices - 4)])
    low = lax.rem(device, 4) < 2
    sent = tuple(jnp.where(low, a, b) for a, b in zip(own, far))
    middle = move(sent, [(i, i ^ 2) for i in range(devices)])
    even = lax.rem(device, 2) == 0
    sent = tuple(jnp.where(even, a, b) for a, b in zip(own, far))
    swap = [(i, i ^ 1) for i in range(devices)]
    first = move(sent, swap)
    second = move(middle, swap)
    return tuple(zip(far, middle, first, second, own))


def on_device(
    queries,
    first_keys,
    first_values,
    second_keys,
    second_values,
    out_weight,
    norm_gain,
    gate_weight,
    up_weight,
    down_weight,
    routes,
    route_weights,
):
    length = queries.shape[0]
    feature_width = queries.shape[1]
    head_count = feature_width // HEAD_DIM
    chunks = math.gcd(head_count // 2, 4)
    chunk_width = feature_width // chunks
    device = lax.axis_index("wide")
    devices = lax.axis_size("wide")
    assert length * 4 == WIN_KEYS and devices % 4 == 0
    full_weight = lax.all_gather(out_weight, "wide", axis=0, tiled=True)
    key_tail, value_tail = lax.ppermute(
        (second_keys[length - TAIL:], second_values[length - TAIL:]),
        "wide",
        [(i, i + 1) for i in range(devices - 1)],
    )
    key_tail = jnp.where(device == 0, second_keys[0:1], key_tail)
    pieces = []
    for chunk in range(chunks):
        cols = slice(chunk * chunk_width, (chunk + 1) * chunk_width)
        key_blocks, value_blocks = spread_blocks(
            first_keys[:, cols], first_values[:, cols], devices, device
        )
        pieces.append(
            attention(queries, key_blocks, value_blocks, key_tail, second_keys,
                      value_tail, second_values, chunk, chunk_width)
        )
    attended = jnp.concatenate(pieces, axis=1)
    model_width = out_weight.shape[1]
    projected32 = jnp.dot(
        attended,
        full_weight,
        preferred_element_type=jnp.float32,
    )
    projected = projected32.astype(jnp.bfloat16)
    wide_proj = projected.astype(jnp.float32)
    normed = (
        wide_proj
        * lax.rsqrt(jnp.mean(wide_proj * wide_proj, axis=1, keepdims=True) + 1e-06)
        * norm_gain
    ).astype(jnp.bfloat16)
    local_experts = gate_weight.shape[0]
    flight = local_experts * devices
    slot_count = flight * CAP
    route_count = routes.shape[1]
    flat_routes = routes.reshape(-1)
    entry = jnp.arange(flat_routes.shape[0], dtype=jnp.int32)
    same = (flat_routes[:, None] == flat_routes[None, :]) & (entry[None, :] < entry[:, None])
    ranking = jnp.sum(same.astype(jnp.int32), axis=1)
    in_flight = flat_routes < flight
    target = jnp.where(in_flight, flat_routes * CAP + ranking, slot_count)
    chooser = target[None, :] == jnp.arange(slot_count, dtype=jnp.int32)[:, None]
    token_chooser = jnp.any(chooser.reshape(slot_count, length, route_count), axis=2)
    outgoing = jnp.dot(
        token_chooser.astype(jnp.bfloat16), normed, preferred_element_type=jnp.float32
    ).astype(jnp.bfloat16)
    outgoing = outgoing.reshape(devices, local_experts, CAP, model_width)
    arrived = lax.all_to_all(outgoing, "wide", split_axis=0, concat_axis=0, tiled=True)
    sources, experts_here, kept_slots, row_width = arrived.shape
    expert_rows = arrived.transpose(1, 0, 2, 3).reshape(
        experts_here, sources * kept_slots, row_width
    )
    gate_proj = jnp.einsum(
        "erd,edf->erf", expert_rows, gate_weight, preferred_element_type=jnp.float32
    )
    upward = jnp.einsum("erd,edf->erf", expert_rows, up_weight, preferred_element_type=jnp.float32)
    hidden = (jax.nn.silu(gate_proj) * upward).astype(jnp.bfloat16)
    result = jnp.einsum(
        "erf,efd->erd", hidden, down_weight, preferred_element_type=jnp.float32
    ).astype(jnp.bfloat16)
    finished = result.reshape(experts_here, sources, kept_slots, row_width).transpose(1, 0, 2, 3)
    returned = lax.all_to_all(finished, "wide", split_axis=0, concat_axis=0, tiled=True).reshape(
        slot_count, model_width
    )
    picked = jnp.take(returned, jnp.minimum(target, slot_count - 1), axis=0).astype(jnp.float32)
    route_scale = jnp.where(in_flight, route_weights.reshape(-1), jnp.float32(0.0))
    expert_sum = jnp.sum(
        (picked * route_scale[:, None]).reshape(length, route_count, model_width), axis=1
    )
    return (wide_proj + expert_sum).astype(jnp.bfloat16)


def solution(mesh):
    in_specs = (
        P(("groups", "wide"), None),
        P(("groups", "wide"), None),
        P(("groups", "wide"), None),
        P(("groups", "wide"), None),
        P(("groups", "wide"), None),
        P("wide", None),
        P(),
        P("wide", None, None),
        P("wide", None, None),
        P("wide", None, None),
        P(("groups", "wide"), None),
        P(("groups", "wide"), None),
    )
    out_specs = P(("groups", "wide"), None)
    return jax.shard_map(
        on_device, mesh=mesh, in_specs=in_specs, out_specs=out_specs, check_vma=False
    )
```

```python
import functools
import math

import jax
import jax.numpy as jnp
from jax import lax
from jax.experimental import pallas as pl
from jax.experimental.pallas import tpu as pltpu
from jax.sharding import PartitionSpec as P

HEAD_DIM = 128
WIN_KEYS = 512
WIN_PAIRS = 12
CAP = 4
TAIL = 16
FAR = -1e30
SCALE = math.log2(math.e) / math.sqrt(HEAD_DIM)


def head_columns(head):
    return pl.ds(pl.multiple_of(head * HEAD_DIM, HEAD_DIM), HEAD_DIM)


def build_masks(device, length, blocks, keys_ext, pair_query, values_ext, alive):
    row = lax.broadcasted_iota(jnp.int32, (length, length), 0)
    col = lax.broadcasted_iota(jnp.int32, (length, length), 1)
    odd = lax.rem(device, 2)
    distances = (blocks - 1, 2, jnp.where(odd == 1, 1, 3), jnp.where(odd == 1, 3, 1), 0)
    for place, distance in enumerate(distances):
        if place == 0:
            admitted = row > col
        elif place == blocks - 1:
            admitted = row <= col
        else:
            admitted = row >= 0
        admitted = admitted & (device >= distance)
        keys_ext[place * length:(place + 1) * length, HEAD_DIM:] = jnp.where(
            admitted, 0.0, FAR
        ).astype(jnp.bfloat16)
    identity = jnp.where(row == col, 1.0, 0.0).astype(jnp.bfloat16)
    for offset in range(WIN_PAIRS):
        pair_query[offset * length:(offset + 1) * length, HEAD_DIM:] = identity
    values_ext[:, HEAD_DIM:] = jnp.ones((blocks * length, HEAD_DIM), jnp.bfloat16)
    ext_row = lax.broadcasted_iota(jnp.int32, alive.shape, 0)
    alive[...] = jnp.where((ext_row >= TAIL) | (device > 0), 1.0, 0.0)


def score_head(head, query_ref, key_blocks, pair_tail_ref, pair_keys_ref,
               keys_ext, pair_query, pair_ext, scores, tops):
    length = query_ref.shape[0]
    blocks = len(key_blocks)
    cols = head_columns(head)
    pair_ext[0:TAIL, :] = pair_tail_ref[:, cols].astype(jnp.float32)
    pair_ext[TAIL:, :] = pair_keys_ref[:, cols].astype(jnp.float32)
    for place, block in enumerate(key_blocks):
        keys_ext[place * length:(place + 1) * length, :HEAD_DIM] = block[:, cols]
    query = query_ref[:, cols].astype(jnp.float32) * SCALE
    for offset in range(WIN_PAIRS):
        pair_query[offset * length:(offset + 1) * length, :HEAD_DIM] = (
            query * pair_ext[TAIL - offset:TAIL - offset + length, :]
        ).astype(jnp.bfloat16)
    top = None
    total = blocks * length
    for start in range(0, total, 256):
        size = min(256, total - start)
        part = lax.dot_general(
            pair_query[...], keys_ext[start:start + size, :],
            (((1,), (1,)), ((), ())), preferred_element_type=jnp.float32,
        )
        scores[:, start:start + size] = part
        for lane in range(0, size, 128):
            for offset in range(WIN_PAIRS):
                tile = part[offset * length:(offset + 1) * length, lane:lane + 128]
                top = tile if top is None else jnp.maximum(top, tile)
    tops[...] = jnp.broadcast_to(jnp.max(top, axis=1, keepdims=True), tops.shape)


def value_head(head, value_blocks, pair_tail_ref, pair_values_ref,
               values_ext, pair_ext, alive, scores, tops, weights, out_ref):
    length = tops.shape[0]
    blocks = len(value_blocks)
    cols = head_columns(head)
    pair_ext[0:TAIL, :] = pair_tail_ref[:, cols].astype(jnp.float32)
    pair_ext[TAIL:, :] = pair_values_ref[:, cols].astype(jnp.float32)
    for place, block in enumerate(value_blocks):
        values_ext[place * length:(place + 1) * length, :HEAD_DIM] = block[:, cols]
    top = tops[...]
    for offset in range(WIN_PAIRS):
        rows = slice(offset * length, (offset + 1) * length)
        for place in range(blocks):
            lanes = slice(place * length, (place + 1) * length)
            weights[rows, lanes] = jnp.exp2((scores[rows, lanes] - top).astype(jnp.bfloat16))
    product = jnp.dot(weights[...], values_ext[...], preferred_element_type=jnp.float32)
    number = jnp.zeros((length, HEAD_DIM), jnp.float32)
    total = jnp.zeros((length, HEAD_DIM), jnp.float32)
    for offset in range(WIN_PAIRS):
        rows = slice(offset * length, (offset + 1) * length)
        near = slice(TAIL - offset, TAIL - offset + length)
        number += product[rows, :HEAD_DIM] * pair_ext[near, :]
        total += product[rows, HEAD_DIM:] * alive[near, :]
    out_ref[:, cols] = (number / total).astype(out_ref.dtype)


def attention_kernel(query, k0, k1, k2, k3, k4, v0, v1, v2, v3, v4,
                     key_tail, pair_keys, value_tail, pair_values, out,
                     keys_ext, pair_query, values_ext, key_ext, value_ext, alive,
                     scores_a, scores_b, tops_a, tops_b, weights):
    length = query.shape[0]
    heads = query.shape[1] // HEAD_DIM
    key_blocks = (k0, k1, k2, k3, k4)
    value_blocks = (v0, v1, v2, v3, v4)
    device = lax.axis_index("wide")
    build_masks(device, length, len(key_blocks), keys_ext, pair_query, values_ext, alive)

    def score(head, scores, tops):
        score_head(head, query, key_blocks, key_tail, pair_keys,
                   keys_ext, pair_query, key_ext, scores, tops)

    def value(head, scores, tops):
        value_head(head, value_blocks, value_tail, pair_values,
                   values_ext, value_ext, alive, scores, tops, weights, out)

    score(0, scores_a, tops_a)

    def pair(step, carry):
        head = step * 2
        score(head + 1, scores_b, tops_b)
        value(head, scores_a, tops_a)
        score(jnp.minimum(head + 2, heads - 1), scores_a, tops_a)
        value(head + 1, scores_b, tops_b)
        return carry

    lax.fori_loop(0, heads // 2, pair, 0)


def attention(query, window, key_tail, pair_keys, value_tail, pair_values,
              chunk, width):
    length = query.shape[0]
    blocks = len(window)
    whole = pl.BlockSpec((length, width), lambda i: (0, chunk))
    sliced = pl.BlockSpec((length, width), lambda i: (0, 0))
    lower = pl.BlockSpec((length, width), lambda i: (1, 0))
    tail = pl.BlockSpec((TAIL, width), lambda i: (0, chunk))
    rows = WIN_PAIRS * length
    keys = blocks * length
    heads = width // HEAD_DIM
    return pl.pallas_call(
        attention_kernel,
        grid=(1,),
        out_shape=jax.ShapeDtypeStruct((length, width), jnp.bfloat16),
        in_specs=[whole] + [sliced] * blocks + [lower] * blocks + [tail, whole, tail, whole],
        out_specs=sliced,
        scratch_shapes=[
            pltpu.VMEM((keys, 2 * HEAD_DIM), jnp.bfloat16),
            pltpu.VMEM((rows, 2 * HEAD_DIM), jnp.bfloat16),
            pltpu.VMEM((keys, 2 * HEAD_DIM), jnp.bfloat16),
            pltpu.VMEM((TAIL + length, HEAD_DIM), jnp.float32),
            pltpu.VMEM((TAIL + length, HEAD_DIM), jnp.float32),
            pltpu.VMEM((TAIL + length, HEAD_DIM), jnp.float32),
            pltpu.VMEM((rows, keys), jnp.float32),
            pltpu.VMEM((rows, keys), jnp.float32),
            pltpu.VMEM((length, HEAD_DIM), jnp.float32),
            pltpu.VMEM((length, HEAD_DIM), jnp.float32),
            pltpu.VMEM((rows, keys), jnp.bfloat16),
        ],
        compiler_params=pltpu.CompilerParams(vmem_limit_bytes=40 * 2**20),
        cost_estimate=pl.CostEstimate(
            flops=heads * 8 * rows * keys * HEAD_DIM,
            bytes_accessed=(2 * blocks + 4) * length * width * 2,
            transcendentals=heads * rows * keys,
        ),
    )(query, *window, *window, key_tail, pair_keys, value_tail, pair_values)


def spread_blocks(own, devices, device, after):
    far = lax.ppermute(own, "wide", [(i, i + 4) for i in range(devices - 4)])
    sent = jnp.where(lax.rem(device, 4) < 2, own, far)
    middle = lax.ppermute(sent, "wide", [(i, i ^ 2) for i in range(devices)])
    sent = jnp.where(lax.rem(device, 2) == 0, own, far)
    if after is not None:
        sent, moved, after = lax.optimization_barrier((sent, middle, after))
    else:
        moved = middle
    swap = [(i, i ^ 1) for i in range(devices)]
    first = lax.ppermute(sent, "wide", swap)
    second = lax.ppermute(moved, "wide", swap)
    return (far, moved, first, second, own), after


def on_device(
    queries,
    first_keys,
    first_values,
    second_keys,
    second_values,
    out_weight,
    norm_gain,
    gate_weight,
    up_weight,
    down_weight,
    routes,
    route_weights,
):
    length = queries.shape[0]
    feature_width = queries.shape[1]
    head_count = feature_width // HEAD_DIM
    chunks = math.gcd(head_count // 2, 4)
    chunk_width = feature_width // chunks
    device = lax.axis_index("wide")
    devices = lax.axis_size("wide")
    assert length * 4 == WIN_KEYS and devices % 4 == 0
    full_weight = lax.all_gather(out_weight, "wide", axis=0, tiled=True)
    key_tail, value_tail = lax.ppermute(
        (second_keys[length - TAIL:], second_values[length - TAIL:]),
        "wide",
        [(i, i + 1) for i in range(devices - 1)],
    )
    key_tail = jnp.where(device == 0, second_keys[0:1], key_tail)
    pieces = []
    for chunk in range(chunks):
        cols = slice(chunk * chunk_width, (chunk + 1) * chunk_width)
        own = jnp.concatenate([first_keys[:, cols], first_values[:, cols]], axis=0)
        after = pieces[chunk - 2] if chunk >= 2 else None
        window, after = spread_blocks(own, devices, device, after)
        if after is not None:
            pieces[chunk - 2] = after
        pieces.append(
            attention(queries, window, key_tail, second_keys,
                      value_tail, second_values, chunk, chunk_width)
        )
    attended = jnp.concatenate(pieces, axis=1)
    model_width = out_weight.shape[1]
    projected32 = jnp.dot(
        attended,
        full_weight,
        preferred_element_type=jnp.float32,
    )
    projected = projected32.astype(jnp.bfloat16)
    wide_proj = projected.astype(jnp.float32)
    normed = (
        wide_proj
        * lax.rsqrt(jnp.mean(wide_proj * wide_proj, axis=1, keepdims=True) + 1e-06)
        * norm_gain
    ).astype(jnp.bfloat16)
    local_experts = gate_weight.shape[0]
    flight = local_experts * devices
    slot_count = flight * CAP
    route_count = routes.shape[1]
    flat_routes = routes.reshape(-1)
    entry = jnp.arange(flat_routes.shape[0], dtype=jnp.int32)
    same = (flat_routes[:, None] == flat_routes[None, :]) & (entry[None, :] < entry[:, None])
    ranking = jnp.sum(same.astype(jnp.int32), axis=1)
    in_flight = flat_routes < flight
    target = jnp.where(in_flight, flat_routes * CAP + ranking, slot_count)
    chooser = target[None, :] == jnp.arange(slot_count, dtype=jnp.int32)[:, None]
    token_chooser = jnp.any(chooser.reshape(slot_count, length, route_count), axis=2)
    outgoing = jnp.dot(
        token_chooser.astype(jnp.bfloat16), normed, preferred_element_type=jnp.float32
    ).astype(jnp.bfloat16)
    outgoing = outgoing.reshape(devices, local_experts, CAP, model_width)
    arrived = lax.all_to_all(outgoing, "wide", split_axis=0, concat_axis=0, tiled=True)
    sources, experts_here, kept_slots, row_width = arrived.shape
    expert_rows = arrived.transpose(1, 0, 2, 3).reshape(
        experts_here, sources * kept_slots, row_width
    )
    gate_proj = jnp.einsum(
        "erd,edf->erf", expert_rows, gate_weight, preferred_element_type=jnp.float32
    )
    upward = jnp.einsum("erd,edf->erf", expert_rows, up_weight, preferred_element_type=jnp.float32)
    hidden = (jax.nn.silu(gate_proj) * upward).astype(jnp.bfloat16)
    result = jnp.einsum(
        "erf,efd->erd", hidden, down_weight, preferred_element_type=jnp.float32
    ).astype(jnp.bfloat16)
    finished = result.reshape(experts_here, sources, kept_slots, row_width).transpose(1, 0, 2, 3)
    returned = lax.all_to_all(finished, "wide", split_axis=0, concat_axis=0, tiled=True).reshape(
        slot_count, model_width
    )
    picked = jnp.take(returned, jnp.minimum(target, slot_count - 1), axis=0).astype(jnp.float32)
    route_scale = jnp.where(in_flight, route_weights.reshape(-1), jnp.float32(0.0))
    expert_sum = jnp.sum(
        (picked * route_scale[:, None]).reshape(length, route_count, model_width), axis=1
    )
    return (wide_proj + expert_sum).astype(jnp.bfloat16)


def solution(mesh):
    in_specs = (
        P(("groups", "wide"), None),
        P(("groups", "wide"), None),
        P(("groups", "wide"), None),
        P(("groups", "wide"), None),
        P(("groups", "wide"), None),
        P("wide", None),
        P(),
        P("wide", None, None),
        P("wide", None, None),
        P("wide", None, None),
        P(("groups", "wide"), None),
        P(("groups", "wide"), None),
    )
    out_specs = P(("groups", "wide"), None)
    return jax.shard_map(
        on_device, mesh=mesh, in_specs=in_specs, out_specs=out_specs, check_vma=False
    )
```
